32 devices in a mesh: fit: 8 (over z, core), orb: 4 (over y, x).
Axes of the slice: x: 2, y: 2, z: 4, core: 2. Of those that a mesh axis runs over, the one named last changes fastest.
Arguments:
- half_ints: bfloat16 [4, 64, 768, 256], P('orb', None, 'fit'), may hold values from -6 to 6
- osv_coef: bfloat16 [4, 64, 256, 64], P('orb', 'fit'), may hold values from -0.09375 to 0.09375
- fit_blocks: int32 [4, 64, 6], P('orb', 'fit'), may hold values from 0 to 468, as said below
- partner_list: int32 [8, 4, 24], P('fit'), may hold values from 0 to 31, as said below
Outputs:
- pair_ints: bfloat16 [4, 64, 24, 4096], P('orb', 'fit')
The draws below stay inside these ranges and needn't reach their ends.
Inputs may be any that keep to these rules, and one draw needn't show every extreme that they name: `fit_blocks`: the 6 block numbers of one orbital are distinct. `partner_list`: entry h * 8 + k names orbital k of the same column in group h. The 24 entries of one list are distinct. Of one list, at most 8 entries name orbitals of any one group, and in every list some group is named exactly 8 times.
All inputs are finite; a program needn't handle non-finite values.
Results may differ from the reference program's by a relative error of at most 0.0055.
Values may be sent and summed in bfloat16 or wider, within the bound.
A program may use at most 64 MiB of HBM per device.

```python
import jax
import jax.numpy as jnp
from jax import lax

AOD = 256
BLK = 128
FBLK = 6
NOSV = 64
NFB = 469
ORB_DEV = 8
NPART = 24
FD = 768
ORBITAL_GROUPS = 4
GROUP_COLUMNS = 8
GRP = 64
CAP = 8


def draw_fit_blocks(key, part):
    key_pool, key_pick = jax.random.split(key)
    pool_size = 2 * FBLK
    scores = jax.random.randint(key_pool, (NFB,), 0, 1 << 20) * 1024 + jnp.arange(NFB, dtype=jnp.int32)
    pool_ids = jnp.argsort(scores)[:pool_size].astype(jnp.int32)
    pick_scores = jax.random.randint(key_pick, (ORBITAL_GROUPS, GRP, pool_size), 0, 1 << 20) * 64 + jnp.arange(pool_size, dtype=jnp.int32)
    chosen_order = jnp.argsort(pick_scores, axis=-1)[..., :FBLK]
    return pool_ids[chosen_order].astype(jnp.int32)


def draw_partner_list(key, part):
    popular_key, key_forced, key_base, key_perm = jax.random.split(key, 4)
    slot_count = ORBITAL_GROUPS * CAP
    slot_positions = jnp.arange(slot_count, dtype=jnp.int32)
    slot_holder = slot_positions // CAP
    popular_boost = jax.random.randint(popular_key, (GROUP_COLUMNS, ORBITAL_GROUPS), 0, 3)
    mandatory_flags = jax.random.randint(key_forced, (GROUP_COLUMNS, ORBITAL_GROUPS), 0, ORBITAL_GROUPS)
    baseline_sample = jax.random.randint(key_base, (GROUP_COLUMNS, ORBITAL_GROUPS, slot_count), 0, 4096)
    holder_boost = popular_boost[:, slot_holder][:, None, :]
    mandatory_boost = (slot_holder[None, None, :] == mandatory_flags[:, :, None]).astype(jnp.int32) * 8
    ranking_score = (baseline_sample + (holder_boost + mandatory_boost) * 4096) * 1024 + slot_positions[None, None, :]
    top_vals, chosen = lax.top_k(ranking_score, NPART)
    owner_group = chosen // CAP
    slot_within = chosen % CAP
    perm_scores = jax.random.randint(key_perm, (GROUP_COLUMNS, ORBITAL_GROUPS, ORBITAL_GROUPS, ORB_DEV), 0, 1 << 20) * 64 + jnp.arange(ORB_DEV, dtype=jnp.int32)
    local_perm = jnp.argsort(perm_scores, axis=-1).astype(jnp.int32).reshape(GROUP_COLUMNS, ORBITAL_GROUPS, ORBITAL_GROUPS * ORB_DEV)
    local_pick = jnp.take_along_axis(local_perm, owner_group * ORB_DEV + slot_within, axis=2)
    return (owner_group * ORB_DEV + local_pick).astype(jnp.int32)


def levels(stream_key, extent, cuts, low, top_value):
    level = 1.0
    for axis_at, shards_of in cuts:
        steps = jax.random.uniform(jax.random.fold_in(jax.random.fold_in(stream_key, 6), axis_at), (shards_of,), jnp.float32, low / len(cuts), top_value / len(cuts))
        level = level * jnp.repeat(jnp.exp(steps), extent[axis_at] // shards_of).reshape((-1,) + (1,) * (len(extent) - 1 - axis_at))
    return level


def noise(rng, shape, spread, bound, cuts=(), kind=jnp.bfloat16):
    gain = levels(rng, shape, cuts, -0.22, 0.18) if cuts else 1.0
    values = jax.random.normal(rng, shape, jnp.float32) * spread * gain
    return jnp.minimum(jnp.maximum(values, -bound), bound).astype(kind)


def setup_inputs(seed: int = 0) -> dict:
    streams_of = jax.random.split(jax.random.key(seed), 5)
    return {
        "half_ints": noise(streams_of[0], (ORBITAL_GROUPS, GRP, FD, AOD), 1.0, 6.0, ((0, 4), (2, 8))),
        "osv_coef": noise(streams_of[1], (ORBITAL_GROUPS, GRP, AOD, NOSV), (AOD * 16) ** -0.5, 0.09375, ((0, 4), (1, 8))),
        "fit_blocks": draw_fit_blocks(jax.random.fold_in(streams_of[4], 71), 0),
        "partner_list": draw_partner_list(jax.random.fold_in(streams_of[4], 71), 0),
    }


def pair_block(own_rows, own_ids, partner_rows, partner_ids):
    matching = (own_ids[None, :, None] == partner_ids[:, None, :]).astype(jnp.float32)
    pieces = partner_rows.astype(jnp.float32).reshape(NPART, NOSV, FBLK, BLK)
    aligned = jnp.einsum('nbc,nxcp->nxbp', matching, pieces).astype(jnp.bfloat16)
    local_rows = own_rows.astype(jnp.float32).reshape(NOSV, FBLK, BLK)
    pair_vals = jnp.einsum('abp,nxbp->nax', local_rows, aligned.astype(jnp.float32))
    return pair_vals.reshape(NPART, NOSV * NOSV).astype(jnp.bfloat16)


def reference(half_ints, osv_coef, fit_blocks, partner_list):
    def project(operand):
        group_rows, group_coef = operand
        return jnp.einsum('rfa,rao->rof', group_rows.astype(jnp.float32), group_coef.astype(jnp.float32)).astype(jnp.bfloat16)

    projected = lax.map(project, (half_ints, osv_coef))
    flat_rows = projected.reshape(ORBITAL_GROUPS * GRP, NOSV, FD)
    flat_blocks = fit_blocks.reshape(ORBITAL_GROUPS * GRP, FBLK)

    def one_orbital(orbital):
        group = orbital // GRP
        row_index = orbital % GRP
        column = row_index // ORB_DEV
        wanted = partner_list[column, group]
        partner_ids = ((wanted // ORB_DEV) * GRP + column * ORB_DEV + wanted % ORB_DEV).astype(jnp.int32)
        return pair_block(flat_rows[orbital], flat_blocks[orbital], flat_rows[partner_ids], flat_blocks[partner_ids])

    result = lax.map(one_orbital, jnp.arange(ORBITAL_GROUPS * GRP, dtype=jnp.int32))
    return result.reshape(ORBITAL_GROUPS, GRP, NPART, NOSV * NOSV)
```

```python
import functools

import jax
import jax.numpy as jnp
from jax import lax
from jax.experimental import pallas as pl
from jax.experimental.pallas import tpu as pltpu
from jax.sharding import PartitionSpec as P

BLK = 128


def pair_kernel(sizes, wanted_ref, index_ref, own_ref, all_ref, out_ref, turned, staged):
    pairs, nosv, fblk, npart = sizes
    orbs = 2 * pairs
    half = nosv // 2
    lanes = 2 * nosv
    row = lax.broadcasted_iota(jnp.int32, (lanes, lanes), 0)
    col = lax.broadcasted_iota(jnp.int32, (lanes, lanes), 1)
    inner = row % nosv
    source = (row // nosv) * nosv + (inner % half) * 2 + inner // half
    order = jnp.where(col == source, 1.0, 0.0).astype(jnp.bfloat16)
    for q in range(pairs):
        flipped = lax.dot_general(
            order, own_ref[q], (((1,), (1,)), ((), ())), preferred_element_type=jnp.float32
        ).astype(jnp.bfloat16)
        for s in range(2):
            for b in range(fblk):
                turned[2 * q + s, b] = flipped[s * nosv:(s + 1) * nosv, b * BLK:(b + 1) * BLK]
            turned[2 * q + s, fblk] = jnp.zeros((nosv, BLK), jnp.bfloat16)

    lane = lax.broadcasted_iota(jnp.int32, (half, lanes), 1)
    low = lane < nosv

    @pl.loop(0, npart)
    def _(n):
        w = wanted_ref[n]
        slab = w // 2
        odd = (w % 2) == 1
        rhs = all_ref[slab]
        lhs = jnp.concatenate(
            [
                jnp.concatenate(
                    [turned[r, index_ref[(w * orbs + r) * fblk + e]] for e in range(fblk)], axis=1
                )
                for r in range(orbs)
            ],
            axis=0,
        )
        vals = jnp.dot(lhs, rhs, preferred_element_type=jnp.float32)
        keep_low = jnp.logical_xor(low, odd)
        for r in range(orbs):
            even_rows = vals[r * nosv:r * nosv + half]
            odd_rows = vals[r * nosv + half:(r + 1) * nosv]
            moved = pltpu.roll(jnp.where(odd, even_rows, odd_rows), nosv, 1)
            kept = jnp.where(odd, odd_rows, even_rows)
            staged[r, pl.ds(n, half, stride=npart), :] = jnp.where(keep_low, kept, moved)

    for r in range(orbs):
        for j in range(half):
            out_ref[r, :, j * lanes:(j + 1) * lanes] = staged[
                r, j * npart:(j + 1) * npart, :
            ].astype(jnp.bfloat16)


def pair_integrals(own, gathered, own_blocks, all_blocks, wanted):
    pairs, depth, lanes = own.shape
    nosv = lanes // 2
    orbs, fblk = own_blocks.shape
    npart = wanted.shape[0]
    count = all_blocks.shape[0]
    hits = all_blocks[:, None, :, None] == own_blocks[None, :, None, :]
    numbers = jnp.arange(fblk, dtype=jnp.int32)
    index = fblk + jnp.sum(jnp.where(hits, numbers - fblk, 0), axis=3, dtype=jnp.int32)
    return pl.pallas_call(
        functools.partial(pair_kernel, (pairs, nosv, fblk, npart)),
        out_shape=jax.ShapeDtypeStruct((orbs, npart, nosv * nosv), jnp.bfloat16),
        in_specs=[
            pl.BlockSpec(memory_space=pltpu.SMEM),
            pl.BlockSpec(memory_space=pltpu.SMEM),
            pl.BlockSpec(memory_space=pltpu.VMEM),
            pl.BlockSpec(memory_space=pltpu.VMEM),
        ],
        out_specs=pl.BlockSpec(memory_space=pltpu.VMEM),
        scratch_shapes=[
            pltpu.VMEM((orbs, fblk + 1, nosv, BLK), jnp.bfloat16),
            pltpu.VMEM((orbs, (nosv // 2) * npart, lanes), jnp.float32),
        ],
        compiler_params=pltpu.CompilerParams(vmem_limit_bytes=48 << 20),
        cost_estimate=pl.CostEstimate(
            flops=2 * npart * orbs * nosv * lanes * depth,
            bytes_accessed=2 * (own.size + gathered.size + orbs * npart * nosv * nosv),
            transcendentals=0,
        ),
    )(wanted, index.reshape(count * orbs * fblk), own, gathered)


def exchange(rows, osv):
    own_ints = lax.all_to_all(rows, "fit", split_axis=0, concat_axis=1, tiled=True)
    orbs, depth = own_ints.shape[:2]
    nosv = osv.shape[-1]
    projected = jnp.einsum(
        "kfa,kao->kfo", own_ints, osv, preferred_element_type=jnp.float32
    ).astype(jnp.bfloat16)
    own = (
        projected.reshape(orbs // 2, 2, depth, nosv)
        .transpose(0, 2, 1, 3)
        .reshape(orbs // 2, depth, 2 * nosv)
    )
    return own, lax.all_gather(own, "orb", axis=0, tiled=True)


def per_device(half_ints, osv_coef, fit_blocks, partner_list):
    own_blocks = fit_blocks[0]
    my_group = lax.axis_index("orb")
    wanted = lax.dynamic_index_in_dim(partner_list[0], my_group, 0, keepdims=False)
    all_blocks = lax.all_gather(own_blocks, "orb", axis=0, tiled=True)
    own, gathered = exchange(half_ints[0], osv_coef[0])
    return pair_integrals(own, gathered, own_blocks, all_blocks, wanted)[None]


def solution(mesh):
    return jax.shard_map(
        per_device,
        mesh=mesh,
        in_specs=(
            P("orb", None, "fit", None),
            P("orb", "fit", None, None),
            P("orb", "fit", None),
            P("fit", None, None),
        ),
        out_specs=P("orb", "fit", None, None),
        check_vma=False,
    )
```

```python
import functools

import jax
import jax.numpy as jnp
from jax import lax
from jax.experimental import pallas as pl
from jax.experimental.pallas import tpu as pltpu
from jax.sharding import PartitionSpec as P

BLK = 128
SLOT = 8
MESH = pl.DeviceIdType.MESH


def pair_kernel(sizes, wanted_ref, index_ref, all_ref, out_ref, turned, staged):
    pairs, nosv, fblk, npart = sizes
    orbs = 2 * pairs
    half = nosv // 2
    lanes = 2 * nosv
    group = lax.axis_index("orb")
    row = lax.broadcasted_iota(jnp.int32, (lanes, lanes), 0)
    col = lax.broadcasted_iota(jnp.int32, (lanes, lanes), 1)
    inner = row % nosv
    source = (row // nosv) * nosv + (inner % half) * 2 + inner // half
    order = jnp.where(col == source, 1.0, 0.0).astype(jnp.bfloat16)
    for q in range(pairs):
        flipped = lax.dot_general(
            order, all_ref[group * pairs + q], (((1,), (1,)), ((), ())), preferred_element_type=jnp.float32
        ).astype(jnp.bfloat16)
        for s in range(2):
            for b in range(fblk):
                turned[2 * q + s, b] = flipped[s * nosv:(s + 1) * nosv, b * BLK:(b + 1) * BLK]
            turned[2 * q + s, fblk] = jnp.zeros((nosv, BLK), jnp.bfloat16)

    lane = lax.broadcasted_iota(jnp.int32, (half, lanes), 1)
    low = lane < nosv

    @pl.loop(0, npart)
    def _(n):
        w = wanted_ref[group, n]
        slab = w // 2
        odd = (w % 2) == 1
        rhs = all_ref[slab]
        lhs = jnp.concatenate(
            [
                jnp.concatenate(
                    [turned[r, index_ref[w, r * SLOT + e]] for e in range(fblk)], axis=1
                )
                for r in range(orbs)
            ],
            axis=0,
        )
        vals = jnp.dot(lhs, rhs, preferred_element_type=jnp.float32)
        keep_low = jnp.logical_xor(low, odd)
        for r in range(orbs):
            even_rows = vals[r * nosv:r * nosv + half]
            odd_rows = vals[r * nosv + half:(r + 1) * nosv]
            moved = pltpu.roll(jnp.where(odd, even_rows, odd_rows), nosv, 1)
            kept = jnp.where(odd, odd_rows, even_rows)
            staged[r, pl.ds(n, half, stride=npart), :] = jnp.where(keep_low, kept, moved)

    for r in range(orbs):
        for j in range(half):
            out_ref[r, :, j * lanes:(j + 1) * lanes] = staged[
                r, j * npart:(j + 1) * npart, :
            ].astype(jnp.bfloat16)


def pair_integrals(gathered, index, lists, orbs, fblk):
    depth, lanes = gathered.shape[1:]
    pairs, nosv, npart = orbs // 2, lanes // 2, lists.shape[1]
    return pl.pallas_call(
        functools.partial(pair_kernel, (pairs, nosv, fblk, npart)),
        out_shape=jax.ShapeDtypeStruct((orbs, npart, nosv * nosv), jnp.bfloat16),
        in_specs=[
            pl.BlockSpec(memory_space=pltpu.SMEM),
            pl.BlockSpec(memory_space=pltpu.SMEM),
            pl.BlockSpec(memory_space=pltpu.VMEM),
        ],
        out_specs=pl.BlockSpec(memory_space=pltpu.VMEM),
        scratch_shapes=[
            pltpu.VMEM((orbs, fblk + 1, nosv, BLK), jnp.bfloat16),
            pltpu.VMEM((orbs, (nosv // 2) * npart, lanes), jnp.float32),
        ],
        compiler_params=pltpu.CompilerParams(vmem_limit_bytes=48 << 20),
        cost_estimate=pl.CostEstimate(
            flops=2 * npart * orbs * nosv * lanes * depth,
            bytes_accessed=2 * (gathered.size + orbs * npart * nosv * nosv),
            transcendentals=0,
        ),
    )(lists, index, gathered)


def match_index(theirs, own, fblk):
    index = jnp.full(theirs.shape, fblk, jnp.int32)
    for b in range(fblk):
        index = jnp.where(theirs == own[b:b + 1, :], b, index)
    return index


def move_kernel(
    columns, osv_ref, tile_ref, own_tile_ref, rows_ref, all_ref, index_ref,
    rows_v, osv_all, stage, tiles,
    rows_sem, osv_send, osv_recv, tile_send, tile_recv, piece_send, piece_recv,
    out_send, out_recv, far_send, far_recv, fblk,
):
    fits = columns
    levels = fits // 2
    pairs, aod, lanes = osv_ref.shape
    orbs = 2 * pairs
    depth = rows_v.shape[1]
    half = pairs // 2
    me = lax.axis_index("fit")
    g = lax.axis_index("orb")
    z, core = me // 2, me % 2
    sib = z * 2 + 1 - core
    y, x = g // 2, g % 2
    sides = (y * 2 + 1 - x, (1 - y) * 2 + x)
    far = (1 - y) * 2 + 1 - x

    def rows_copy(c):
        here = pl.ds(c * orbs, orbs)
        return pltpu.make_async_copy(rows_ref.at[here], rows_v.at[here], rows_sem.at[c])

    for c in range(fits):
        rows_copy(c).start()

    barrier = pltpu.get_barrier_semaphore()
    for step in range(1, fits):
        pl.semaphore_signal(barrier, inc=1, device_id={"fit": (me + step) % fits}, device_id_type=MESH)
    for peer in (*sides, far):
        pl.semaphore_signal(barrier, inc=1, device_id={"orb": peer}, device_id_type=MESH)
    pl.semaphore_wait(barrier, fits - 1 + 3)

    def osv_copy(shard, way, target, source=None):
        return pltpu.make_async_remote_copy(
            src_ref=osv_all.at[shard] if source is None else source,
            dst_ref=osv_all.at[shard],
            send_sem=osv_send.at[way, shard],
            recv_sem=osv_recv.at[shard],
            device_id={"fit": target},
            device_id_type=MESH,
        )

    def slab(h, d, first, count):
        return all_ref.at[
            pl.ds(h * pairs + first, count), pl.ds(pl.multiple_of(d * depth, 16), depth), :
        ]

    def piece_copy(c):
        return pltpu.make_async_remote_copy(
            src_ref=stage.at[c],
            dst_ref=slab(g, me, 0, pairs),
            send_sem=piece_send.at[c],
            recv_sem=piece_recv.at[me],
            device_id={"fit": c},
            device_id_type=MESH,
        )

    def piece_arrival(d):
        return pltpu.make_async_remote_copy(
            src_ref=stage.at[d],
            dst_ref=slab(g, d, 0, pairs),
            send_sem=piece_send.at[d],
            recv_sem=piece_recv.at[d],
            device_id={"fit": d},
            device_id_type=MESH,
        )

    def out_copy(d, way, h):
        part = slab(h, d, 0, pairs)
        return pltpu.make_async_remote_copy(
            src_ref=part, dst_ref=part,
            send_sem=out_send.at[way, d], recv_sem=out_recv.at[way, d],
            device_id={"orb": sides[way]}, device_id_type=MESH,
        )

    def far_copy(d, way, h):
        part = slab(h, d, half * (1 - way), half)
        return pltpu.make_async_remote_copy(
            src_ref=part, dst_ref=part,
            send_sem=far_send.at[way, d], recv_sem=far_recv.at[way, d],
            device_id={"orb": sides[way]}, device_id_type=MESH,
        )

    def tile_copy(number, peer, slot):
        return pltpu.make_async_remote_copy(
            src_ref=tile_ref, dst_ref=tiles.at[slot],
            send_sem=tile_send.at[number], recv_sem=tile_recv.at[slot],
            device_id={"orb": peer}, device_id_type=MESH,
        )

    low = lax.broadcasted_iota(jnp.int32, (depth, lanes), 1) < lanes // 2

    def project(c, osv, q):
        lhs = rows_v[pl.ds(c * orbs + 2 * q, 2)].reshape(2 * depth, aod)
        vals = jnp.dot(lhs, osv, preferred_element_type=jnp.float32)
        return jnp.where(low, vals[:depth], vals[depth:]).astype(jnp.bfloat16)

    def project_and_send(c):
        osv_copy(c, 0, sib).wait_recv()
        rows_copy(c).wait()
        for q in range(pairs):
            stage[c, q] = project(c, osv_all[c, q], q)
        piece_copy(c).start()

    def within(level):
        return jnp.logical_and(level >= 0, level < levels)

    def at_distance(j, action):
        if j == 0:
            action(me)
            action(sib)
        else:
            for s in (1, -1):
                @pl.when(within(z + s * j))
                def _():
                    action((z + s * j) * 2 + core)
                    action((z + s * j) * 2 + 1 - core)

    def spread(d):
        out_copy(d, 0, g).start()
        out_copy(d, 1, g).start()

    def take_and_spread(d):
        piece_arrival(d).wait_recv()
        spread(d)

    def relay(d):
        out_copy(d, 0, sides[0]).wait_recv()
        far_copy(d, 1, sides[0]).start()
        out_copy(d, 1, sides[1]).wait_recv()
        far_copy(d, 0, sides[1]).start()

    for way, s in ((0, 1), (1, -1)):
        @pl.when(within(z + s))
        def _():
            osv_copy(me, way, me + 2 * s, osv_ref).start()
    osv_copy(me, 2, sib, osv_ref).start()
    for number, peer in enumerate((*sides, far)):
        tile_copy(number, peer, g).start()

    rows_copy(me).wait()
    for q in range(pairs):
        all_ref[g * pairs + q, pl.ds(pl.multiple_of(me * depth, 16), depth), :] = project(
            me, osv_ref[q], q
        )
    spread(me)
    project_and_send(sib)

    for j in range(1, levels):
        for way, s in ((1, 1), (0, -1)):
            @pl.when(within(z + s * j))
            def _():
                shard = (z + s * j) * 2 + core
                osv_copy(shard, way, sib).wait_recv()

                @pl.when(within(z - s))
                def _():
                    osv_copy(shard, way, me - 2 * s).start()
                osv_copy(shard, 2, sib).start()
                rows_copy(shard).wait()
                for q in range(pairs):
                    stage[shard, q] = project(shard, osv_all[shard, q], q)
                piece_copy(shard).start()
        for s in (1, -1):
            @pl.when(within(z + s * j))
            def _():
                project_and_send((z + s * j) * 2 + 1 - core)
        if j == 1:
            take_and_spread(sib)
            for number, peer in enumerate((*sides, far)):
                tile_copy(number, peer, peer).wait_recv()
            tiles[g] = tile_ref[...]
            for h in range(tiles.shape[0]):
                index_ref[h * orbs:(h + 1) * orbs, :] = match_index(
                    tiles[h], own_tile_ref[...], fblk
                )
        else:
            at_distance(j - 1, take_and_spread)
            at_distance(j - 2, relay)
    at_distance(levels - 1, take_and_spread)
    if levels > 1:
        at_distance(levels - 2, relay)
    at_distance(levels - 1, relay)

    for d in range(fits):
        far_copy(d, 1, far).wait_recv()
        far_copy(d, 0, far).wait_recv()
    for d in range(fits):
        for way in range(2):
            out_copy(d, way, g).wait_send()
            far_copy(d, way, sides[1 - way]).wait_send()

        @pl.when(d != me)
        def _():
            piece_copy(d).wait_send()
    for number, peer in enumerate((*sides, far)):
        tile_copy(number, peer, g).wait_send()
    for way, s in ((0, 1), (1, -1)):
        @pl.when(within(z + s))
        def _():
            osv_copy(me, way, me + 2 * s, osv_ref).wait_send()
    osv_copy(me, 2, sib, osv_ref).wait_send()
    for j in range(1, levels):
        for way, s in ((1, 1), (0, -1)):
            @pl.when(within(z + s * j))
            def _():
                shard = (z + s * j) * 2 + core

                @pl.when(within(z - s))
                def _():
                    osv_copy(shard, way, me - 2 * s).wait_send()
                osv_copy(shard, 2, sib).wait_send()


def move(rows, osv, tile, own_tile, fits, fblk):
    pairs, aod, lanes = osv.shape
    orbs = 2 * pairs
    depth = rows.shape[1]
    groups = 4
    dma = pltpu.SemaphoreType.DMA
    full = pl.BlockSpec(memory_space=pltpu.VMEM)

    def kernel(*refs):
        move_kernel(fits, *refs, fblk)

    return pl.pallas_call(
        kernel,
        out_shape=(
            jax.ShapeDtypeStruct((groups * pairs, fits * depth, lanes), jnp.bfloat16),
            jax.ShapeDtypeStruct((groups * orbs, tile.shape[1]), jnp.int32),
        ),
        in_specs=[full, full, full, pl.BlockSpec(memory_space=pl.ANY)],
        out_specs=(full, full),
        scratch_shapes=[
            pltpu.VMEM(rows.shape, jnp.bfloat16),
            pltpu.VMEM((fits, pairs, aod, lanes), jnp.bfloat16),
            pltpu.VMEM((fits, pairs, depth, lanes), jnp.bfloat16),
            pltpu.VMEM((groups, *tile.shape), jnp.int32),
            dma((fits,)),
            dma((3, fits)), dma((fits,)),
            dma((3,)), dma((groups,)),
            dma((fits,)), dma((fits,)),
            dma((2, fits)), dma((2, fits)),
            dma((2, fits)), dma((2, fits)),
        ],
        compiler_params=pltpu.CompilerParams(
            collective_id=0, has_side_effects=True, vmem_limit_bytes=48 << 20
        ),
        cost_estimate=pl.CostEstimate(
            flops=2 * rows.size * lanes, bytes_accessed=4 * rows.size, transcendentals=0
        ),
    )(osv, tile, own_tile, rows)


def exchange(rows, osv):
    own_ints = lax.all_to_all(rows, "fit", split_axis=0, concat_axis=1, tiled=True)
    projected = jnp.einsum(
        "kfa,kao->kfo", own_ints, osv, preferred_element_type=jnp.float32
    ).astype(jnp.bfloat16)
    return lax.all_gather(side_by_side(projected), "orb", axis=0, tiled=True)


def side_by_side(pieces):
    count, rows, width = pieces.shape
    return (
        pieces.reshape(count // 2, 2, rows, width)
        .transpose(0, 2, 1, 3)
        .reshape(count // 2, rows, 2 * width)
    )


def per_device(sizes, half_ints, osv_coef, fit_blocks, partner_list):
    fits, groups = sizes
    rows, osv, blocks = half_ints[0], osv_coef[0], fit_blocks[0]
    orbs, fblk = blocks.shape
    width = -(-orbs * SLOT // 128) * 128
    padded = jnp.pad(blocks, ((0, 0), (0, SLOT - fblk)), constant_values=-1)
    tile = jnp.tile(padded, (1, width // SLOT))
    own_tile = jnp.pad(
        jnp.repeat(padded.T, SLOT, axis=1), ((0, 0), (0, width - orbs * SLOT)), constant_values=-2
    )
    if groups == 4 and fits % 2 == 0 and rows.shape[1] % 16 == 0:
        gathered, index = move(rows, side_by_side(osv), tile, own_tile, fits, fblk)
    else:
        gathered = exchange(rows, osv)
        index = match_index(lax.all_gather(tile, "orb", axis=0, tiled=True), own_tile, fblk)
    return pair_integrals(gathered, index, partner_list[0], orbs, fblk)[None]


def solution(mesh):
    return jax.shard_map(
        functools.partial(per_device, (mesh.shape["fit"], mesh.shape["orb"])),
        mesh=mesh,
        in_specs=(
            P("orb", None, "fit", None),
            P("orb", "fit", None, None),
            P("orb", "fit", None),
            P("fit", None, None),
        ),
        out_specs=P("orb", "fit", None, None),
        check_vma=False,
    )
```

```python
import functools

import jax
import jax.numpy as jnp
from jax import lax
from jax.experimental import pallas as pl
from jax.experimental.pallas import tpu as pltpu
from jax.sharding import PartitionSpec as P

BLK = 128
SLOT = 8
MESH = pl.DeviceIdType.MESH


def pair_kernel(sizes, wanted_ref, index_ref, all_ref, out_ref, turned, staged):
    pairs, nosv, fblk, npart = sizes
    orbs = 2 * pairs
    half = nosv // 2
    lanes = 2 * nosv
    group = lax.axis_index("orb")
    row = lax.broadcasted_iota(jnp.int32, (lanes, lanes), 0)
    col = lax.broadcasted_iota(jnp.int32, (lanes, lanes), 1)
    inner = row % nosv
    source = (row // nosv) * nosv + (inner % half) * 2 + inner // half
    order = jnp.where(col == source, 1.0, 0.0).astype(jnp.bfloat16)
    for q in range(pairs):
        flipped = lax.dot_general(
            order, all_ref[group * pairs + q], (((1,), (1,)), ((), ())), preferred_element_type=jnp.float32
        ).astype(jnp.bfloat16)
        for s in range(2):
            for b in range(fblk):
                turned[2 * q + s, b] = flipped[s * nosv:(s + 1) * nosv, b * BLK:(b + 1) * BLK]
            turned[2 * q + s, fblk] = jnp.zeros((nosv, BLK), jnp.bfloat16)

    lane = lax.broadcasted_iota(jnp.int32, (half, lanes), 1)
    low = lane < nosv

    @pl.loop(0, npart, unroll=12)
    def _(n):
        w = wanted_ref[group, n]
        slab = w // 2
        odd = (w % 2) == 1
        rhs = all_ref[slab]
        lhs = jnp.concatenate(
            [
                jnp.concatenate(
                    [turned[r, index_ref[w, r * SLOT + e]] for e in range(fblk)], axis=1
                )
                for r in range(orbs)
            ],
            axis=0,
        )
        vals = jnp.dot(lhs, rhs, preferred_element_type=jnp.float32)
        keep_low = jnp.logical_xor(low, odd)
        for r in range(orbs):
            even_rows = vals[r * nosv:r * nosv + half]
            odd_rows = vals[r * nosv + half:(r + 1) * nosv]
            moved = pltpu.roll(jnp.where(odd, even_rows, odd_rows), nosv, 1)
            kept = jnp.where(odd, odd_rows, even_rows)
            staged[r, pl.ds(n, half, stride=npart), :] = jnp.where(keep_low, kept, moved)

    for r in range(orbs):
        for j in range(half):
            out_ref[r, :, j * lanes:(j + 1) * lanes] = staged[
                r, j * npart:(j + 1) * npart, :
            ].astype(jnp.bfloat16)


def pair_integrals(gathered, index, lists, orbs, fblk):
    depth, lanes = gathered.shape[1:]
    pairs, nosv, npart = orbs // 2, lanes // 2, lists.shape[1]
    return pl.pallas_call(
        functools.partial(pair_kernel, (pairs, nosv, fblk, npart)),
        out_shape=jax.ShapeDtypeStruct((orbs, npart, nosv * nosv), jnp.bfloat16),
        in_specs=[
            pl.BlockSpec(memory_space=pltpu.SMEM),
            pl.BlockSpec(memory_space=pltpu.SMEM),
            pl.BlockSpec(memory_space=pltpu.VMEM),
        ],
        out_specs=pl.BlockSpec(memory_space=pltpu.VMEM),
        scratch_shapes=[
            pltpu.VMEM((orbs, fblk + 1, nosv, BLK), jnp.bfloat16),
            pltpu.VMEM((orbs, (nosv // 2) * npart, lanes), jnp.float32),
        ],
        compiler_params=pltpu.CompilerParams(vmem_limit_bytes=48 << 20),
        cost_estimate=pl.CostEstimate(
            flops=2 * npart * orbs * nosv * lanes * depth,
            bytes_accessed=2 * (gathered.size + orbs * npart * nosv * nosv),
            transcendentals=0,
        ),
    )(lists, index, gathered)


def match_index(theirs, own, fblk):
    index = jnp.full(theirs.shape, fblk, jnp.int32)
    for b in range(fblk):
        index = jnp.where(theirs == own[b:b + 1, :], b, index)
    return index


def move_kernel(
    columns, osv_ref, tile_ref, own_tile_ref, rows_ref, all_ref, index_ref,
    rows_v, osv_all, stage, tiles,
    rows_sem, osv_send, osv_recv, tile_send, tile_recv, piece_send, piece_recv,
    out_send, out_recv, far_send, far_recv, fblk,
):
    fits = columns
    levels = fits // 2
    pairs, aod, lanes = osv_ref.shape
    orbs = 2 * pairs
    depth = rows_v.shape[1]
    half = pairs // 2
    me = lax.axis_index("fit")
    g = lax.axis_index("orb")
    z, core = me // 2, me % 2
    sib = z * 2 + 1 - core
    y, x = g // 2, g % 2
    sides = (y * 2 + 1 - x, (1 - y) * 2 + x)
    far = (1 - y) * 2 + 1 - x

    def rows_copy(c):
        here = pl.ds(c * orbs, orbs)
        return pltpu.make_async_copy(rows_ref.at[here], rows_v.at[here], rows_sem.at[c])

    for c in range(fits):
        rows_copy(c).start()

    barrier = pltpu.get_barrier_semaphore()
    for step in range(1, fits):
        pl.semaphore_signal(barrier, inc=1, device_id={"fit": (me + step) % fits}, device_id_type=MESH)
    for peer in (*sides, far):
        pl.semaphore_signal(barrier, inc=1, device_id={"orb": peer}, device_id_type=MESH)
    pl.semaphore_wait(barrier, fits - 1 + 3)

    parts = 2
    size = pairs // parts

    class Parts:
        def __init__(self, *copies):
            self.copies = copies

        def start(self):
            for copy in self.copies:
                copy.start()

        def wait_recv(self):
            for copy in self.copies:
                copy.wait_recv()

        def wait_send(self):
            for copy in self.copies:
                copy.wait_send()

    def osv_copy(shard, way, target, source=None):
        return Parts(*(osv_part(shard, way, target, source, p) for p in range(parts)))

    def osv_part(shard, way, target, source, p):
        some = pl.ds(p * size, size)
        return pltpu.make_async_remote_copy(
            src_ref=osv_all.at[shard, some] if source is None else source.at[some],
            dst_ref=osv_all.at[shard, some],
            send_sem=osv_send.at[way, shard, p],
            recv_sem=osv_recv.at[shard, p],
            device_id={"fit": target},
            device_id_type=MESH,
        )

    def slab(h, d, first, count):
        return all_ref.at[
            pl.ds(h * pairs + first, count), pl.ds(pl.multiple_of(d * depth, 16), depth), :
        ]

    def piece_copy(c):
        return pltpu.make_async_remote_copy(
            src_ref=stage.at[c],
            dst_ref=slab(g, me, 0, pairs),
            send_sem=piece_send.at[c],
            recv_sem=piece_recv.at[me],
            device_id={"fit": c},
            device_id_type=MESH,
        )

    def piece_arrival(d):
        return pltpu.make_async_remote_copy(
            src_ref=stage.at[d],
            dst_ref=slab(g, d, 0, pairs),
            send_sem=piece_send.at[d],
            recv_sem=piece_recv.at[d],
            device_id={"fit": d},
            device_id_type=MESH,
        )

    def out_copy(d, way, h):
        part = slab(h, d, 0, pairs)
        return pltpu.make_async_remote_copy(
            src_ref=part, dst_ref=part,
            send_sem=out_send.at[way, d], recv_sem=out_recv.at[way, d],
            device_id={"orb": (*sides, far)[way]}, device_id_type=MESH,
        )

    def far_copy(d, way, h):
        part = slab(h, d, half * (1 - way), half)
        return pltpu.make_async_remote_copy(
            src_ref=part, dst_ref=part,
            send_sem=far_send.at[way, d], recv_sem=far_recv.at[way, d],
            device_id={"orb": sides[way]}, device_id_type=MESH,
        )

    def tile_copy(number, peer, slot):
        return pltpu.make_async_remote_copy(
            src_ref=tile_ref, dst_ref=tiles.at[slot],
            send_sem=tile_send.at[number], recv_sem=tile_recv.at[slot],
            device_id={"orb": peer}, device_id_type=MESH,
        )

    low = lax.broadcasted_iota(jnp.int32, (depth, lanes), 1) < lanes // 2

    def project(c, osv, q):
        lhs = rows_v[pl.ds(c * orbs + 2 * q, 2)].reshape(2 * depth, aod)
        vals = jnp.dot(lhs, osv, preferred_element_type=jnp.float32)
        return jnp.where(low, vals[:depth], vals[depth:]).astype(jnp.bfloat16)

    def project_and_send(c):
        osv_copy(c, 0, sib).wait_recv()
        rows_copy(c).wait()
        for q in range(pairs):
            stage[c, q] = project(c, osv_all[c, q], q)
        piece_copy(c).start()

    def within(level):
        return jnp.logical_and(level >= 0, level < levels)

    def at_distance(j, action):
        if j == 0:
            action(me, 0)
            action(sib, 0)
        else:
            for s in (1, -1):
                @pl.when(within(z + s * j))
                def _():
                    action((z + s * j) * 2 + core, j)
                    action((z + s * j) * 2 + 1 - core, j)

    cutoff = 0

    def spread(d, j):
        if j >= cutoff:
            out_copy(d, 2, g).start()
        out_copy(d, 0, g).start()
        out_copy(d, 1, g).start()

    def take_and_spread(d, j):
        piece_arrival(d).wait_recv()
        spread(d, j)

    def relay(d, j):
        if j < cutoff:
            out_copy(d, 0, sides[0]).wait_recv()
            far_copy(d, 1, sides[0]).start()
            out_copy(d, 1, sides[1]).wait_recv()
            far_copy(d, 0, sides[1]).start()

    def last_arrivals(d, j):
        if j < cutoff:
            far_copy(d, 1, far).wait_recv()
            far_copy(d, 0, far).wait_recv()
        else:
            for way, h in enumerate((*sides, far)):
                out_copy(d, way, h).wait_recv()

    def last_sends(d, j):
        for way in range(2):
            out_copy(d, way, g).wait_send()
            if j < cutoff:
                far_copy(d, way, sides[1 - way]).wait_send()
        if j >= cutoff:
            out_copy(d, 2, g).wait_send()

    for way, s in ((0, 1), (1, -1)):
        @pl.when(within(z + s))
        def _():
            osv_copy(me, way, me + 2 * s, osv_ref).start()
    osv_copy(me, 2, sib, osv_ref).start()
    for number, peer in enumerate((*sides, far)):
        tile_copy(number, peer, g).start()

    rows_copy(me).wait()
    for q in range(pairs):
        all_ref[g * pairs + q, pl.ds(pl.multiple_of(me * depth, 16), depth), :] = project(
            me, osv_ref[q], q
        )
    spread(me, 0)
    project_and_send(sib)

    def project_at(j):
        for s in (1, -1):
            @pl.when(within(z + s * j))
            def _():
                shard = (z + s * j) * 2 + core
                rows_copy(shard).wait()
                for q in range(pairs):
                    stage[shard, q] = project(shard, osv_all[shard, q], q)
                piece_copy(shard).start()
        for s in (1, -1):
            @pl.when(within(z + s * j))
            def _():
                project_and_send((z + s * j) * 2 + 1 - core)

    for j in range(1, levels):
        for p in range(parts):
            for way, s in ((1, 1), (0, -1)):
                @pl.when(within(z + s * j))
                def _():
                    shard = (z + s * j) * 2 + core
                    osv_part(shard, way, sib, None, p).wait_recv()

                    @pl.when(within(z - s))
                    def _():
                        osv_part(shard, way, me - 2 * s, None, p).start()
                    osv_part(shard, 2, sib, None, p).start()
        if j == 1:
            project_at(j)
            piece_arrival(sib).wait_recv()
            spread(sib, 0)
            for number, peer in enumerate((*sides, far)):
                tile_copy(number, peer, peer).wait_recv()
            tiles[g] = tile_ref[...]
            for h in range(tiles.shape[0]):
                index_ref[h * orbs:(h + 1) * orbs, :] = match_index(
                    tiles[h], own_tile_ref[...], fblk
                )
            relay(me, 0)
        elif j == 2:
            at_distance(j - 1, take_and_spread)
            relay(sib, 0)
            project_at(j)
        else:
            project_at(j)
            at_distance(j - 1, take_and_spread)
            at_distance(j - 2, relay)
    at_distance(levels - 1, take_and_spread)
    if levels > 2:
        at_distance(levels - 2, relay)
    if levels == 2:
        relay(sib, 0)
    at_distance(levels - 1, relay)

    for j in range(levels):
        at_distance(j, last_arrivals)
    for j in range(levels):
        at_distance(j, last_sends)
    for d in range(fits):
        @pl.when(d != me)
        def _():
            piece_copy(d).wait_send()
    for number, peer in enumerate((*sides, far)):
        tile_copy(number, peer, g).wait_send()
    for way, s in ((0, 1), (1, -1)):
        @pl.when(within(z + s))
        def _():
            osv_copy(me, way, me + 2 * s, osv_ref).wait_send()
    osv_copy(me, 2, sib, osv_ref).wait_send()
    for j in range(1, levels):
        for way, s in ((1, 1), (0, -1)):
            @pl.when(within(z + s * j))
            def _():
                shard = (z + s * j) * 2 + core

                @pl.when(within(z - s))
                def _():
                    osv_copy(shard, way, me - 2 * s).wait_send()
                osv_copy(shard, 2, sib).wait_send()


def move(rows, osv, tile, own_tile, fits, fblk):
    pairs, aod, lanes = osv.shape
    orbs = 2 * pairs
    depth = rows.shape[1]
    groups = 4
    dma = pltpu.SemaphoreType.DMA
    full = pl.BlockSpec(memory_space=pltpu.VMEM)

    def kernel(*refs):
        move_kernel(fits, *refs, fblk)

    return pl.pallas_call(
        kernel,
        out_shape=(
            jax.ShapeDtypeStruct((groups * pairs, fits * depth, lanes), jnp.bfloat16),
            jax.ShapeDtypeStruct((groups * orbs, tile.shape[1]), jnp.int32),
        ),
        in_specs=[full, full, full, pl.BlockSpec(memory_space=pl.ANY)],
        out_specs=(full, full),
        scratch_shapes=[
            pltpu.VMEM(rows.shape, jnp.bfloat16),
            pltpu.VMEM((fits, pairs, aod, lanes), jnp.bfloat16),
            pltpu.VMEM((fits, pairs, depth, lanes), jnp.bfloat16),
            pltpu.VMEM((groups, *tile.shape), jnp.int32),
            dma((fits,)),
            dma((3, fits, 2)), dma((fits, 2)),
            dma((3,)), dma((groups,)),
            dma((fits,)), dma((fits,)),
            dma((3, fits)), dma((3, fits)),
            dma((2, fits)), dma((2, fits)),
        ],
        compiler_params=pltpu.CompilerParams(
            collective_id=0, has_side_effects=True, vmem_limit_bytes=48 << 20
        ),
        cost_estimate=pl.CostEstimate(
            flops=2 * rows.size * lanes, bytes_accessed=4 * rows.size, transcendentals=0
        ),
    )(osv, tile, own_tile, rows)


def exchange(rows, osv):
    own_ints = lax.all_to_all(rows, "fit", split_axis=0, concat_axis=1, tiled=True)
    projected = jnp.einsum(
        "kfa,kao->kfo", own_ints, osv, preferred_element_type=jnp.float32
    ).astype(jnp.bfloat16)
    return lax.all_gather(side_by_side(projected), "orb", axis=0, tiled=True)


def side_by_side(pieces):
    count, rows, width = pieces.shape
    return (
        pieces.reshape(count // 2, 2, rows, width)
        .transpose(0, 2, 1, 3)
        .reshape(count // 2, rows, 2 * width)
    )


def per_device(sizes, half_ints, osv_coef, fit_blocks, partner_list):
    fits, groups = sizes
    rows, osv, blocks = half_ints[0], osv_coef[0], fit_blocks[0]
    orbs, fblk = blocks.shape
    width = -(-orbs * SLOT // 128) * 128
    padded = jnp.pad(blocks, ((0, 0), (0, SLOT - fblk)), constant_values=-1)
    tile = jnp.tile(padded, (1, width // SLOT))
    own_tile = jnp.pad(
        jnp.repeat(padded.T, SLOT, axis=1), ((0, 0), (0, width - orbs * SLOT)), constant_values=-2
    )
    if groups == 4 and fits % 2 == 0 and rows.shape[1] % 16 == 0:
        gathered, index = move(rows, side_by_side(osv), tile, own_tile, fits, fblk)
    else:
        gathered = exchange(rows, osv)
        index = match_index(lax.all_gather(tile, "orb", axis=0, tiled=True), own_tile, fblk)
    return pair_integrals(gathered, index, partner_list[0], orbs, fblk)[None]


def solution(mesh):
    return jax.shard_map(
        functools.partial(per_device, (mesh.shape["fit"], mesh.shape["orb"])),
        mesh=mesh,
        in_specs=(
            P("orb", None, "fit", None),
            P("orb", "fit", None, None),
            P("orb", "fit", None),
            P("fit", None, None),
        ),
        out_specs=P("orb", "fit", None, None),
        check_vma=False,
    )
```
